32 devices in a mesh: seq: 4 (over y, x), head: 8 (over z, core).
Axes of the slice: x: 2, y: 2, z: 4, core: 2. Of those that a mesh axis runs over, the one named last changes fastest.
Arguments:
- signal: bfloat16 [8192, 5120], P('seq', 'head'), may hold values from -0.119628906 to 0.119628906
- log_decay: float32 [80, 8192], P('head', 'seq'), may hold values from -0.6 to 0
- b_matrix: bfloat16 [8192, 128], P('seq'), may hold values from -6 to 6
- c_matrix: bfloat16 [8192, 128], P('seq'), may hold values from -0.5 to 0.5
- out_grad: bfloat16 [8192, 5120], P('seq', 'head'), may hold values from -0.4 to 0.4
Outputs:
- output: float32 [8192, 5120], P('seq', 'head')
- grad_signal: float32 [8192, 5120], P('seq', 'head')
- grad_decay: float32 [80, 8192], P('head', 'seq')
- grad_b: float32 [8192, 128], P(('seq', 'head'))
- grad_c: float32 [8192, 128], P(('seq', 'head'))
- head_grads: float32 [2, 80], P(None, 'head')
The draws below stay inside these ranges and needn't reach their ends.
All inputs are finite; a program needn't handle non-finite values.
Results may differ from the reference program's by a relative error of at most 0.012.
Values sent between devices are 32-bit elements; how exact they have to be, the bound alone decides.
A program may use at most 192 MiB of HBM per device.

```python
import math
import jax
import jax.numpy as jnp
from jax import lax

ATTENTION_WAYS = 80
HEAD_DIM = 64
STATE = 128
SPAN = 256
STRAND_SPAN = 8192


def draw_log_decay(key, part):
    keys = jax.random.split(jax.random.fold_in(key, 11), 6)
    slow_share = 0.5
    slow = jax.random.bernoulli(keys[0], slow_share, (ATTENTION_WAYS,))
    whole = jnp.exp(jax.random.uniform(keys[1], (ATTENTION_WAYS,), jnp.float32, math.log(1.15), math.log(1.35)))
    slow_rate = whole / STRAND_SPAN
    fast_rate = 1.0 / (SPAN * jax.random.uniform(keys[2], (ATTENTION_WAYS,), jnp.float32, 0.12, 0.2))
    forgetting_speed = jnp.where(slow, slow_rate, fast_rate)
    approximate_guess = jnp.exp(jax.random.uniform(keys[3], (ATTENTION_WAYS, STRAND_SPAN), jnp.float32, math.log(0.5), math.log(1.5)))
    steady_rate = jnp.minimum(forgetting_speed[:, None] * approximate_guess, 0.15)
    symbol_offsets = jax.random.permutation(keys[4], STRAND_SPAN)[:3]
    layer_tiers = jax.random.uniform(keys[5], (3, ATTENTION_WAYS), jnp.float32, 0.22, 0.28)
    symbol_location = jnp.arange(STRAND_SPAN)
    packet_clusters = jnp.zeros((ATTENTION_WAYS, STRAND_SPAN), jnp.float32)
    for portion_number in range(3):
        packet_clusters = packet_clusters + (symbol_location[None, :] == symbol_offsets[portion_number]).astype(jnp.float32) * layer_tiers[portion_number][:, None]
    return -(steady_rate + packet_clusters)


def draw_out_grad(key, part):
    keyed = jax.random.fold_in(key, 23)
    symbol_location = jnp.arange(STRAND_SPAN).astype(jnp.float32)
    ramp = 1.0 + 2.0 * symbol_location / max(STRAND_SPAN - 1, 1)
    noise = jnp.clip(jax.random.normal(keyed, (STRAND_SPAN, ATTENTION_WAYS * HEAD_DIM), jnp.float32), -6.0, 6.0)
    return (0.02 * noise * ramp[:, None]).astype(jnp.bfloat16)


def block_levels(own_key, dims, pieces, smallest, top_value):
    def one(dim, shards_of):
        draws = jax.random.uniform(jax.random.fold_in(jax.random.fold_in(own_key, 6), dim), (shards_of,), jnp.float32, smallest / len(pieces), top_value / len(pieces))
        return jnp.repeat(jnp.exp(draws), dims[dim] // shards_of).reshape((-1,) + (1,) * (len(dims) - dim - 1))

    factor_of = one(*pieces[0])
    for cut in pieces[1:]:
        factor_of = factor_of * one(*cut)
    return factor_of


def bell_draw(own_key, shape, scale, limit, cuts=(), kind=jnp.bfloat16):
    factor_of = block_levels(own_key, shape, cuts, -0.22, 0.18) if cuts else 1.0
    values = jax.random.normal(own_key, shape, jnp.float32) * scale * factor_of
    return jnp.minimum(jnp.maximum(values, -limit), limit).astype(kind)


def setup_inputs(seed: int = 0) -> dict:
    key_list = jax.random.split(jax.random.key(seed), 6)
    signal = bell_draw(key_list[0], (STRAND_SPAN, ATTENTION_WAYS * HEAD_DIM), 0.02, 0.119628906, ((0, 4), (1, 8)))
    log_decay = draw_log_decay(jax.random.fold_in(key_list[5], 71), 0)
    b_matrix = bell_draw(key_list[2], (STRAND_SPAN, STATE), 1.0, 6.0, ((0, 4),))
    c_matrix = bell_draw(key_list[3], (STRAND_SPAN, STATE), STATE ** -0.5, 0.5, ((0, 4),))
    out_grad = draw_out_grad(jax.random.fold_in(key_list[5], 71), 0)
    return dict(signal=signal, log_decay=log_decay, b_matrix=b_matrix, c_matrix=c_matrix, out_grad=out_grad)


highest = lax.Precision.HIGHEST

def span_step(state, inputs):
    values, decays, b_block, c_block = inputs
    cumulated = jnp.cumsum(decays, axis=1)
    length = decays.shape[1]
    lower = jnp.tril(jnp.ones((length, length), dtype=bool))
    spread = cumulated[:, :, None] - cumulated[:, None, :]
    weights = jnp.where(lower[None], jnp.exp(jnp.where(lower[None], spread, 0.0)), 0.0)
    b_half = b_block.astype(jnp.bfloat16)
    c_half = c_block.astype(jnp.bfloat16)
    scores = jnp.dot(c_half, b_half.T, preferred_element_type=jnp.float32)
    mixing = (weights * scores[None]).astype(jnp.bfloat16)
    inner = jnp.einsum('hij,jhp->ihp', mixing, values.astype(jnp.bfloat16), preferred_element_type=jnp.float32)
    carried = jnp.einsum('in,hpn->ihp', c_block, state, precision=highest) * jnp.exp(cumulated).T[:, :, None]
    last_sum = cumulated[:, -1]
    tails = jnp.exp(last_sum[:, None] - cumulated)
    scaled = (values * tails.T[:, :, None]).astype(jnp.bfloat16)
    update = jnp.einsum('jhp,jn->hpn', scaled, b_half, preferred_element_type=jnp.float32)
    state = jnp.exp(last_sum)[:, None, None] * state + update
    return (state, inner + carried)

def forward(values, decays, b_full, c_full):
    total = values.shape[0]
    heads = decays.shape[0]
    width = values.shape[1] // heads
    blocks = total // SPAN
    shaped = values.reshape(total, heads, width)
    stacked = shaped.reshape(blocks, SPAN, heads, width)
    decay_blocks = decays.reshape(heads, blocks, SPAN).transpose(1, 0, 2)
    b_blocks = b_full.reshape(blocks, SPAN, b_full.shape[1])
    c_blocks = c_full.reshape(blocks, SPAN, c_full.shape[1])
    start = jnp.zeros((heads, width, b_full.shape[1]), values.dtype)
    _, outputs = lax.scan(span_step, start, (stacked, decay_blocks, b_blocks, c_blocks))
    result = outputs.reshape(total, heads, width) + shaped
    return result.reshape(total, heads * width)

def reference(signal, log_decay, b_matrix, c_matrix, out_grad):
    values = signal.astype(jnp.float32)
    b_full = b_matrix.astype(jnp.float32)
    c_full = c_matrix.astype(jnp.float32)
    grad_full = out_grad.astype(jnp.float32)
    result, pullback = jax.vjp(forward, values, log_decay, b_full, c_full)
    grad_values, grad_decay, grad_b, grad_c = pullback(grad_full)
    total = values.shape[0]
    heads = log_decay.shape[0]
    width = values.shape[1] // heads
    skip_grad = lax.optimization_barrier(jnp.sum(grad_full.reshape(total, heads, width) * values.reshape(total, heads, width), axis=(0, 2)))
    rate_grad = lax.optimization_barrier(jnp.sum(grad_decay * log_decay, axis=1))
    head_grads = jnp.stack([skip_grad, rate_grad])
    return (result, grad_values, grad_decay, grad_b, grad_c, head_grads)
```

```python
import functools

import jax
import jax.numpy as jnp
from jax import lax
from jax.experimental import pallas as pl
from jax.experimental.pallas import tpu as pltpu
from jax.sharding import PartitionSpec as P

SPAN = 256
F32 = jnp.float32
BF16 = jnp.bfloat16
NN = (((1,), (0,)), ((), ()))
NT = (((1,), (1,)), ((), ()))
TN = (((0,), (0,)), ((), ()))


def mm(left, right, dims):
    return lax.dot_general(left, right, dims, preferred_element_type=F32)


def sums(left, right):
    return jnp.dot(left, right, precision=lax.Precision.HIGHEST, preferred_element_type=F32)


def indices():
    rows = lax.broadcasted_iota(jnp.int32, (SPAN, SPAN), 0)
    columns = lax.broadcasted_iota(jnp.int32, (SPAN, SPAN), 1)
    return rows, columns


def states_kernel(heads, width, x_ref, dy_ref, a_ref, b_ref, c_ref,
                  xt_ref, dyt_ref, cum_ref, entry_ref, before_ref, packed_ref, sum_ref):
    k = pl.program_id(0)
    size = heads * width

    @pl.when(k == 0)
    def _():
        packed_ref[...] = jnp.zeros_like(packed_ref)
        sum_ref[...] = jnp.zeros_like(sum_ref)

    x_t = x_ref[...].astype(F32).T
    dy_t = dy_ref[...].astype(F32).T
    xt_ref[...] = x_t.astype(BF16)
    dyt_ref[...] = dy_t.astype(BF16)
    rows, columns = indices()
    cum = sums(a_ref[...], (rows <= columns).astype(F32))
    cum_ref[...] = cum
    last = cum[:, SPAN - 1:]
    head_decay = jnp.exp(cum)
    tail = jnp.exp(last - cum)
    scaled, weighted = [], []
    for h in range(heads):
        part = slice(h * width, (h + 1) * width)
        scaled.append((x_t[part] * tail[h:h + 1]).astype(BF16))
        weighted.append((dy_t[part] * head_decay[h:h + 1]).astype(BF16))
    update = mm(jnp.concatenate(scaled, axis=0), b_ref[...], NN)
    own = mm(jnp.concatenate(weighted, axis=0), c_ref[...], NN)
    before = sum_ref[...]
    before_ref[0] = jnp.exp(before)
    entry_ref[0] = packed_ref[:size]
    for h in range(heads):
        part = slice(h * width, (h + 1) * width)
        later = slice(size + h * width, size + (h + 1) * width)
        packed_ref[part] = packed_ref[part] * jnp.exp(last[h:h + 1]) + update[part]
        packed_ref[later] = packed_ref[later] + jnp.exp(before[h:h + 1]) * own[part]
    sum_ref[...] = before + last
    packed_ref[2 * size:2 * size + heads] = before + last


def core_kernel(heads, width, xt_ref, dyt_ref, a_ref, cum_ref, b_ref, c_ref,
                local_ref, before_ref, entry_ref, after_ref,
                y_ref, gx_ref, ga_ref, gbc_ref, params_ref,
                adj_ref, gs_ref, st_ref, scaled_ref, weighted_ref, yt_ref, gxt_ref):
    k = pl.program_id(0)
    state_size = b_ref.shape[1]

    @pl.when(k == 0)
    def _():
        adj_ref[...] = after_ref[...]
        params_ref[...] = jnp.zeros_like(params_ref)

    rows, columns = indices()
    lower = rows <= columns
    cum = cum_ref[...]
    last = cum[:, SPAN - 1:]
    head_decay = jnp.exp(cum)
    tail = jnp.exp(last - cum)
    whole = jnp.exp(last)
    before = before_ref[0]
    cum_columns = jnp.concatenate(
        [cum, jnp.zeros((-heads % 8, SPAN), F32)] if heads % 8 else [cum], axis=0).T
    b, c = b_ref[...], c_ref[...]
    scores = mm(b, c, NT)
    for h in range(heads):
        part = slice(h * width, (h + 1) * width)
        st_ref[part] = local_ref[0, part] + before[h:h + 1] * entry_ref[part]
    state_half = st_ref[...].astype(BF16)
    adj_half = adj_ref[...].astype(BF16)
    carried_all = mm(state_half, c, NT)
    scaled_grad_all = mm(adj_half, b, NT)
    gain, loss, skip, edge = [], [], [], []
    for h in range(heads):
        part = slice(h * width, (h + 1) * width)
        weights = jnp.where(lower, jnp.exp(cum[h:h + 1] - cum_columns[:, h:h + 1]), 0.0)
        mixing = (weights * scores).astype(BF16)
        x_half, dy_half = xt_ref[part], dyt_ref[part]
        inner = mm(x_half, mixing, NN)
        back = mm(dy_half, mixing, NT)
        mixing_grad = mm(x_half, dy_half, TN)
        piece = weights * mixing_grad
        if h == 0:
            gs_ref[...] = piece
        else:
            gs_ref[...] += piece
        x, dy = x_half.astype(F32), dy_half.astype(F32)
        core = inner + carried_all[part] * head_decay[h:h + 1]
        yt_ref[part] = core + x
        tailed = scaled_grad_all[part] * tail[h:h + 1]
        gxt_ref[part] = back + tailed + dy
        scaled_ref[part] = (x * tail[h:h + 1]).astype(BF16)
        weighted_ref[part] = (dy * head_decay[h:h + 1]).astype(BF16)
        gain.append(jnp.sum(dy * core - x * back, axis=0, keepdims=True))
        loss.append(jnp.sum(x * tailed, axis=0, keepdims=True))
        skip.append(jnp.sum(x * dy, axis=0, keepdims=True))
        products = jnp.sum(st_ref[part] * adj_ref[part], axis=0, keepdims=True)
        edge.append(jnp.sum(products, axis=1, keepdims=True))
    y_ref[...] = yt_ref[...].T
    gx_ref[...] = gxt_ref[...].T
    grad = (sums(jnp.concatenate(gain, axis=0), (rows >= columns).astype(F32))
            + sums(jnp.concatenate(loss, axis=0), (rows < columns).astype(F32))
            + whole * jnp.concatenate(edge, axis=0))
    ga_ref[...] = grad
    params_ref[0] += jnp.concatenate(skip, axis=0)
    params_ref[1] += grad * a_ref[...]
    gs_half = gs_ref[...].astype(BF16)
    gbc_ref[:, :state_size] = mm(gs_half, c, NN) + mm(scaled_ref[...], adj_half, TN)
    gbc_ref[:, state_size:] = mm(gs_half, b, TN) + mm(weighted_ref[...], state_half, TN)
    own = mm(weighted_ref[...], c, NN)
    for h in range(heads):
        part = slice(h * width, (h + 1) * width)
        adj_ref[part] = adj_ref[part] * whole[h:h + 1] + own[part]


def shards(signal, log_decay, b_matrix, c_matrix, out_grad):
    length, size = signal.shape
    heads = log_decay.shape[0]
    width = size // heads
    n = b_matrix.shape[1]
    blocks = length // SPAN
    padded = -(-(2 * size + heads) // 8) * 8
    shape = jax.ShapeDtypeStruct
    params = pltpu.CompilerParams(vmem_limit_bytes=56 * 2**20)

    token = pl.BlockSpec((SPAN, size), lambda k: (k, 0))
    flat = pl.BlockSpec((size, SPAN), lambda k: (0, k))
    decay = pl.BlockSpec((heads, SPAN), lambda k: (0, k))
    maps = pl.BlockSpec((SPAN, n), lambda k: (k, 0))
    xt, dyt, cum, local, before, packed = pl.pallas_call(
        functools.partial(states_kernel, heads, width),
        grid=(blocks,),
        in_specs=[token, token, decay, maps, maps],
        out_specs=[flat, flat, decay,
                   pl.BlockSpec((1, size, n), lambda k: (k, 0, 0)),
                   pl.BlockSpec((1, heads, n), lambda k: (k, 0, 0)),
                   pl.BlockSpec((padded, n), lambda k: (0, 0))],
        out_shape=[shape((size, length), BF16), shape((size, length), BF16),
                   shape((heads, length), F32), shape((blocks, size, n), F32),
                   shape((blocks, heads, n), F32), shape((padded, n), F32)],
        scratch_shapes=[pltpu.VMEM((heads, n), F32)],
        compiler_params=params,
    )(signal, out_grad, log_decay, b_matrix, c_matrix)

    count, mine = lax.axis_size("seq"), lax.axis_index("seq")
    pieces = lax.all_gather(packed, "seq")
    totals = pieces[:, 2 * size:2 * size + heads, 0]
    states = pieces[:, :size].reshape(count, heads, width, n)
    adjoints = pieces[:, size:2 * size].reshape(count, heads, width, n)
    place = jnp.arange(count)
    mid = place[None, :]
    ahead = (mid > place[:, None]) & (mid < mine)
    behind = (mid < place[:, None]) & (mid > mine)
    gap_in = jnp.sum(jnp.where(ahead[:, :, None], totals[None], 0.0), axis=1)
    gap_out = jnp.sum(jnp.where(behind[:, :, None], totals[None], 0.0), axis=1)
    weight_in = jnp.where((place < mine)[:, None], jnp.exp(gap_in), 0.0)
    weight_out = jnp.where((place > mine)[:, None], jnp.exp(gap_out), 0.0)
    entry = jnp.sum(weight_in[:, :, None, None] * states, axis=0).reshape(size, n)
    after = jnp.sum(weight_out[:, :, None, None] * adjoints, axis=0).reshape(size, n)

    end = blocks - 1
    token = pl.BlockSpec((SPAN, size), lambda k: (end - k, 0))
    flat = pl.BlockSpec((size, SPAN), lambda k: (0, end - k))
    decay = pl.BlockSpec((heads, SPAN), lambda k: (0, end - k))
    maps = pl.BlockSpec((SPAN, n), lambda k: (end - k, 0))
    edge = pl.BlockSpec((size, n), lambda k: (0, 0))
    y, gx, ga, gbc, sums_out = pl.pallas_call(
        functools.partial(core_kernel, heads, width),
        grid=(blocks,),
        in_specs=[flat, flat, decay, decay, maps, maps,
                  pl.BlockSpec((1, size, n), lambda k: (end - k, 0, 0)),
                  pl.BlockSpec((1, heads, n), lambda k: (end - k, 0, 0)),
                  edge, edge],
        out_specs=[token, token, decay,
                   pl.BlockSpec((SPAN, 2 * n), lambda k: (end - k, 0)),
                   pl.BlockSpec((2, heads, SPAN), lambda k: (0, 0, 0))],
        out_shape=[shape((length, size), F32), shape((length, size), F32),
                   shape((heads, length), F32), shape((length, 2 * n), F32),
                   shape((2, heads, SPAN), F32)],
        scratch_shapes=[pltpu.VMEM((size, n), F32), pltpu.VMEM((SPAN, SPAN), F32),
                        pltpu.VMEM((size, n), F32), pltpu.VMEM((size, SPAN), BF16),
                        pltpu.VMEM((size, SPAN), BF16), pltpu.VMEM((size, SPAN), F32),
                        pltpu.VMEM((size, SPAN), F32)],
        compiler_params=params,
    )(xt, dyt, log_decay, cum, b_matrix, c_matrix, local, before, entry, after)

    shared = lax.psum_scatter(gbc, "head", scatter_dimension=0, tiled=True)
    head_grads = lax.psum(jnp.sum(sums_out, axis=2), "seq")
    return y, gx, ga, shared[:, :n], shared[:, n:], head_grads


def solution(mesh):
    in_specs = (
        P("seq", "head"),
        P("head", "seq"),
        P("seq", None),
        P("seq", None),
        P("seq", "head"),
    )
    out_specs = (
        P("seq", "head"),
        P("seq", "head"),
        P("head", "seq"),
        P(("seq", "head"), None),
        P(("seq", "head"), None),
        P(None, "head"),
    )
    return jax.shard_map(shards, mesh=mesh, in_specs=in_specs, out_specs=out_specs, check_vma=False)
```

```python
import functools

import jax
import jax.numpy as jnp
from jax import lax
from jax.experimental import pallas as pl
from jax.experimental.pallas import tpu as pltpu
from jax.sharding import PartitionSpec as P

SPAN = 256
F32 = jnp.float32
BF16 = jnp.bfloat16
NN = (((1,), (0,)), ((), ()))
NT = (((1,), (1,)), ((), ()))
TN = (((0,), (0,)), ((), ()))


def mm(left, right, dims):
    return lax.dot_general(left, right, dims, preferred_element_type=F32)


def sums(left, right):
    return jnp.dot(left, right, precision=lax.Precision.HIGHEST, preferred_element_type=F32)


def indices():
    rows = lax.broadcasted_iota(jnp.int32, (SPAN, SPAN), 0)
    columns = lax.broadcasted_iota(jnp.int32, (SPAN, SPAN), 1)
    return rows, columns


def states_kernel(heads, width, x_ref, dy_ref, a_ref, b_ref, c_ref,
                  xt_ref, dyt_ref, cum_ref, entry_ref, before_ref, packed_ref, sum_ref):
    k = pl.program_id(0)
    size = heads * width

    @pl.when(k == 0)
    def _():
        packed_ref[...] = jnp.zeros_like(packed_ref)
        sum_ref[...] = jnp.zeros_like(sum_ref)

    x_t = x_ref[...].astype(F32).T
    dy_t = dy_ref[...].astype(F32).T
    xt_ref[...] = x_t.astype(BF16)
    dyt_ref[...] = dy_t.astype(BF16)
    rows, columns = indices()
    cum = sums(a_ref[...], (rows <= columns).astype(F32))
    cum_ref[...] = cum
    last = cum[:, SPAN - 1:]
    head_decay = jnp.exp(cum)
    tail = jnp.exp(last - cum)
    scaled, weighted = [], []
    for h in range(heads):
        part = slice(h * width, (h + 1) * width)
        scaled.append((x_t[part] * tail[h:h + 1]).astype(BF16))
        weighted.append((dy_t[part] * head_decay[h:h + 1]).astype(BF16))
    update = mm(jnp.concatenate(scaled, axis=0), b_ref[...], NN)
    own = mm(jnp.concatenate(weighted, axis=0), c_ref[...], NN)
    before = sum_ref[...]
    before_ref[0] = jnp.exp(before)
    entry_ref[0] = packed_ref[:size]
    for h in range(heads):
        part = slice(h * width, (h + 1) * width)
        later = slice(size + h * width, size + (h + 1) * width)
        packed_ref[part] = packed_ref[part] * jnp.exp(last[h:h + 1]) + update[part]
        packed_ref[later] = packed_ref[later] + jnp.exp(before[h:h + 1]) * own[part]
    sum_ref[...] = before + last
    packed_ref[2 * size:2 * size + heads] = before + last


def local_kernel(heads, width, xt_ref, dyt_ref, cum_ref, b_ref, c_ref,
                 inner_ref, back_ref, gain_ref, gbc_ref, skip_ref, gs_ref):
    state_size = b_ref.shape[1]

    @pl.when(pl.program_id(0) == 0)
    def _():
        skip_ref[...] = jnp.zeros_like(skip_ref)

    rows, columns = indices()
    lower = rows <= columns
    cum = cum_ref[...]
    cum_columns = jnp.concatenate(
        [cum, jnp.zeros((-heads % 8, SPAN), F32)] if heads % 8 else [cum], axis=0).T
    b, c = b_ref[...], c_ref[...]
    scores = mm(b, c, NT)
    gain, skip = [], []
    for h in range(heads):
        part = slice(h * width, (h + 1) * width)
        weights = jnp.where(lower, jnp.exp(cum[h:h + 1] - cum_columns[:, h:h + 1]), 0.0)
        mixing = (weights * scores).astype(BF16)
        x_half, dy_half = xt_ref[part], dyt_ref[part]
        inner = mm(x_half, mixing, NN)
        back = mm(dy_half, mixing, NT)
        piece = weights * mm(x_half, dy_half, TN)
        if h == 0:
            gs_ref[...] = piece
        else:
            gs_ref[...] += piece
        x, dy = x_half.astype(F32), dy_half.astype(F32)
        inner_ref[part] = inner
        back_ref[part] = back
        gain.append(jnp.sum(dy * inner - x * back, axis=0, keepdims=True))
        skip.append(jnp.sum(x * dy, axis=0, keepdims=True))
    gain_ref[...] = jnp.concatenate(gain, axis=0)
    skip_ref[...] += jnp.concatenate(skip, axis=0)
    gs_half = gs_ref[...].astype(BF16)
    gbc_ref[:, :state_size] = mm(gs_half, c, NN)
    gbc_ref[:, state_size:] = mm(gs_half, b, TN)


def maps_kernel(heads, width, xt_ref, dyt_ref, cum_ref, c_ref, local_ref, before_ref,
                entry_ref, after_ref, part_ref, gbc_ref, state_ref, adjoint_ref, edge_ref,
                adj_ref, st_ref, scaled_ref, weighted_ref):
    state_size = c_ref.shape[1]

    @pl.when(pl.program_id(0) == 0)
    def _():
        adj_ref[...] = after_ref[...]

    cum = cum_ref[...]
    last = cum[:, SPAN - 1:]
    head_decay = jnp.exp(cum)
    tail = jnp.exp(last - cum)
    whole = jnp.exp(last)
    before = before_ref[0]
    edge = []
    for h in range(heads):
        part = slice(h * width, (h + 1) * width)
        state = local_ref[0, part] + before[h:h + 1] * entry_ref[part]
        st_ref[part] = state.astype(BF16)
        products = jnp.sum(state * adj_ref[part], axis=0, keepdims=True)
        edge.append(jnp.sum(products, axis=1, keepdims=True) * whole[h:h + 1])
        scaled_ref[part] = (xt_ref[part].astype(F32) * tail[h:h + 1]).astype(BF16)
        weighted_ref[part] = (dyt_ref[part].astype(F32) * head_decay[h:h + 1]).astype(BF16)
    state_half = st_ref[...]
    adj_half = adj_ref[...].astype(BF16)
    state_ref[0] = state_half
    adjoint_ref[0] = adj_half
    edge_ref[0] = jnp.broadcast_to(jnp.concatenate(edge, axis=0), edge_ref.shape[1:])
    gbc_ref[:, :state_size] = part_ref[:, :state_size] + mm(scaled_ref[...], adj_half, TN)
    gbc_ref[:, state_size:] = part_ref[:, state_size:] + mm(weighted_ref[...], state_half, TN)
    own = mm(weighted_ref[...], c_ref[...], NN)
    for h in range(heads):
        part = slice(h * width, (h + 1) * width)
        adj_ref[part] = adj_ref[part] * whole[h:h + 1] + own[part]


def output_kernel(heads, width, xt_ref, dyt_ref, a_ref, cum_ref, b_ref, c_ref, inner_ref, back_ref,
                  gain_ref, state_ref, adjoint_ref, edge_ref,
                  y_ref, gx_ref, ga_ref, rate_ref, yt_ref, gxt_ref):
    @pl.when(pl.program_id(0) == 0)
    def _():
        rate_ref[...] = jnp.zeros_like(rate_ref)

    rows, columns = indices()
    cum = cum_ref[...]
    last = cum[:, SPAN - 1:]
    head_decay = jnp.exp(cum)
    tail = jnp.exp(last - cum)
    carried_all = mm(state_ref[0], c_ref[...], NT)
    scaled_grad_all = mm(adjoint_ref[0], b_ref[...], NT)
    gain, loss = [], []
    for h in range(heads):
        part = slice(h * width, (h + 1) * width)
        x, dy = xt_ref[part].astype(F32), dyt_ref[part].astype(F32)
        carried = carried_all[part] * head_decay[h:h + 1]
        tailed = scaled_grad_all[part] * tail[h:h + 1]
        yt_ref[part] = inner_ref[part] + carried + x
        gxt_ref[part] = back_ref[part] + tailed + dy
        gain.append(jnp.sum(dy * carried, axis=0, keepdims=True))
        loss.append(jnp.sum(x * tailed, axis=0, keepdims=True))
    y_ref[...] = yt_ref[...].T
    gx_ref[...] = gxt_ref[...].T
    grad = (sums(gain_ref[...] + jnp.concatenate(gain, axis=0), (rows >= columns).astype(F32))
            + sums(jnp.concatenate(loss, axis=0), (rows < columns).astype(F32))
            + edge_ref[0][:, :1])
    ga_ref[...] = grad
    rate_ref[...] += grad * a_ref[...]


def gathered(packed, heads, width, n):
    size = heads * width
    count, mine = lax.axis_size("seq"), lax.axis_index("seq")
    pieces = lax.all_gather(packed, "seq")
    totals = pieces[:, 2 * size:2 * size + heads, 0]
    states = pieces[:, :size].reshape(count, heads, width, n)
    adjoints = pieces[:, size:2 * size].reshape(count, heads, width, n)
    place = jnp.arange(count)
    mid = place[None, :]
    ahead = (mid > place[:, None]) & (mid < mine)
    behind = (mid < place[:, None]) & (mid > mine)
    gap_in = jnp.sum(jnp.where(ahead[:, :, None], totals[None], 0.0), axis=1)
    gap_out = jnp.sum(jnp.where(behind[:, :, None], totals[None], 0.0), axis=1)
    weight_in = jnp.where((place < mine)[:, None], jnp.exp(gap_in), 0.0)
    weight_out = jnp.where((place > mine)[:, None], jnp.exp(gap_out), 0.0)
    entry = jnp.sum(weight_in[:, :, None, None] * states, axis=0).reshape(size, n)
    after = jnp.sum(weight_out[:, :, None, None] * adjoints, axis=0).reshape(size, n)
    return entry, after


def exchanged(packed, heads, width, n):
    size = heads * width
    mine = lax.axis_index("seq")
    state = jnp.concatenate([packed[:size], packed[2 * size:]], axis=0)
    adjoint = packed[size:]
    by_x = lax.ppermute(jnp.where(mine % 2 == 0, state, adjoint), "seq",
                        [(0, 1), (1, 0), (2, 3), (3, 2)])
    by_y = lax.ppermute(jnp.where(mine < 2, state, adjoint), "seq",
                        [(0, 2), (2, 0), (1, 3), (3, 1)])
    far = (lax.ppermute(by_y, "seq", [(0, 1), (3, 2)])
           + lax.ppermute(by_x, "seq", [(1, 3), (2, 0)]))

    def cut(value):
        return value[:size].reshape(heads, width, n), value[size:size + heads, :1, None]

    (near, near_sum), (side, side_sum), (last, last_sum) = cut(by_x), cut(by_y), cut(far)
    whole = near + jnp.exp(near_sum) * side + jnp.exp(near_sum + side_sum) * last
    double = last + jnp.exp(last_sum) * side
    zero = jnp.zeros_like(near)
    entry = jnp.where(mine == 0, zero, jnp.where(mine == 1, near, jnp.where(mine == 2, double, whole)))
    after = jnp.where(mine == 3, zero, jnp.where(mine == 2, near, jnp.where(mine == 1, double, whole)))
    return entry.reshape(size, n), after.reshape(size, n)


def shards(signal, log_decay, b_matrix, c_matrix, out_grad):
    length, size = signal.shape
    heads = log_decay.shape[0]
    width = size // heads
    n = b_matrix.shape[1]
    blocks = length // SPAN
    padded = -(-(2 * size + heads) // 8) * 8
    shape = jax.ShapeDtypeStruct
    params = pltpu.CompilerParams(vmem_limit_bytes=56 * 2**20)

    token = pl.BlockSpec((SPAN, size), lambda k: (k, 0))
    flat = pl.BlockSpec((size, SPAN), lambda k: (0, k))
    decay = pl.BlockSpec((heads, SPAN), lambda k: (0, k))
    maps = pl.BlockSpec((SPAN, n), lambda k: (k, 0))
    xt, dyt, cum, local, before, packed = pl.pallas_call(
        functools.partial(states_kernel, heads, width),
        grid=(blocks,),
        in_specs=[token, token, decay, maps, maps],
        out_specs=[flat, flat, decay,
                   pl.BlockSpec((1, size, n), lambda k: (k, 0, 0)),
                   pl.BlockSpec((1, heads, n), lambda k: (k, 0, 0)),
                   pl.BlockSpec((padded, n), lambda k: (0, 0))],
        out_shape=[shape((size, length), BF16), shape((size, length), BF16),
                   shape((heads, length), F32), shape((blocks, size, n), F32),
                   shape((blocks, heads, n), F32), shape((padded, n), F32)],
        scratch_shapes=[pltpu.VMEM((heads, n), F32)],
        compiler_params=params,
    )(signal, out_grad, log_decay, b_matrix, c_matrix)

    def grad_cost(micros):
        return pl.CostEstimate(flops=int(micros * 1.0e9), bytes_accessed=int(micros * 3.0e6),
                               transcendentals=0)

    per_block = pl.BlockSpec((1, heads, n), lambda k: (k, 0, 0))
    pair = pl.BlockSpec((SPAN, 2 * n), lambda k: (k, 0))
    once = pl.BlockSpec((heads, SPAN), lambda k: (0, 0))
    inner, back, gain, local_maps, skip = pl.pallas_call(
        functools.partial(local_kernel, heads, width),
        grid=(blocks,),
        in_specs=[flat, flat, decay, maps, maps],
        out_specs=[flat, flat, decay, pair, once],
        out_shape=[shape((size, length), F32), shape((size, length), F32),
                   shape((heads, length), F32), shape((length, 2 * n), F32),
                   shape((heads, SPAN), F32)],
        scratch_shapes=[pltpu.VMEM((SPAN, SPAN), F32)],
        compiler_params=params, cost_estimate=grad_cost(18),
    )(xt, dyt, cum, b_matrix, c_matrix)

    exchange = exchanged if lax.axis_size("seq") == 4 else gathered
    entry, after = exchange(packed, heads, width, n)

    end = blocks - 1
    r_flat = pl.BlockSpec((size, SPAN), lambda k: (0, end - k))
    r_state = pl.BlockSpec((1, size, n), lambda k: (end - k, 0, 0))
    r_block = pl.BlockSpec((1, heads, n), lambda k: (end - k, 0, 0))
    r_pair = pl.BlockSpec((SPAN, 2 * n), lambda k: (end - k, 0))
    edge_spec = pl.BlockSpec((size, n), lambda k: (0, 0))
    gbc, state_half, adj_half, edge = pl.pallas_call(
        functools.partial(maps_kernel, heads, width),
        grid=(blocks,),
        in_specs=[r_flat, r_flat, pl.BlockSpec((heads, SPAN), lambda k: (0, end - k)),
                  pl.BlockSpec((SPAN, n), lambda k: (end - k, 0)), r_state, r_block,
                  edge_spec, edge_spec, r_pair],
        out_specs=[r_pair, r_state, r_state, r_block],
        out_shape=[shape((length, 2 * n), F32), shape((blocks, size, n), BF16),
                   shape((blocks, size, n), BF16), shape((blocks, heads, n), F32)],
        scratch_shapes=[pltpu.VMEM((size, n), F32), pltpu.VMEM((size, n), BF16),
                        pltpu.VMEM((size, SPAN), BF16), pltpu.VMEM((size, SPAN), BF16)],
        compiler_params=params, cost_estimate=grad_cost(6),
    )(xt, dyt, cum, c_matrix, local, before, entry, after, local_maps)

    shared = lax.psum_scatter(gbc, "head", scatter_dimension=0, tiled=True)

    state_spec = pl.BlockSpec((1, size, n), lambda k: (k, 0, 0))
    y, gx, ga, rate = pl.pallas_call(
        functools.partial(output_kernel, heads, width),
        grid=(blocks,),
        in_specs=[flat, flat, decay, decay, maps, maps, flat, flat, decay,
                  state_spec, state_spec, per_block],
        out_specs=[token, token, decay, once],
        out_shape=[shape((length, size), F32), shape((length, size), F32),
                   shape((heads, length), F32), shape((heads, SPAN), F32)],
        scratch_shapes=[pltpu.VMEM((size, SPAN), F32), pltpu.VMEM((size, SPAN), F32)],
        compiler_params=params, cost_estimate=grad_cost(14),
    )(xt, dyt, log_decay, cum, b_matrix, c_matrix, inner, back, gain, state_half, adj_half, edge)

    head_grads = lax.psum(jnp.stack([jnp.sum(skip, axis=1), jnp.sum(rate, axis=1)]), "seq")
    return y, gx, ga, shared[:, :n], shared[:, n:], head_grads


def solution(mesh):
    in_specs = (
        P("seq", "head"),
        P("head", "seq"),
        P("seq", None),
        P("seq", None),
        P("seq", "head"),
    )
    out_specs = (
        P("seq", "head"),
        P("seq", "head"),
        P("head", "seq"),
        P(("seq", "head"), None),
        P(("seq", "head"), None),
        P(None, "head"),
    )
    return jax.shard_map(shards, mesh=mesh, in_specs=in_specs, out_specs=out_specs, check_vma=False)
```

```python
import functools

import jax
import jax.numpy as jnp
from jax import lax
from jax.experimental import pallas as pl
from jax.experimental.pallas import tpu as pltpu
from jax.sharding import PartitionSpec as P

SPAN = 256
F32 = jnp.float32
BF16 = jnp.bfloat16
NN = (((1,), (0,)), ((), ()))
NT = (((1,), (1,)), ((), ()))
TN = (((0,), (0,)), ((), ()))


def mm(left, right, dims):
    return lax.dot_general(left, right, dims, preferred_element_type=F32)


def sums(left, right):
    return jnp.dot(left, right, precision=lax.Precision.HIGHEST, preferred_element_type=F32)


def indices():
    rows = lax.broadcasted_iota(jnp.int32, (SPAN, SPAN), 0)
    columns = lax.broadcasted_iota(jnp.int32, (SPAN, SPAN), 1)
    return rows, columns


def states_kernel(heads, width, role_ref, x_ref, dy_ref, a_ref, b_ref, c_ref,
                  xt_ref, dyt_ref, cum_ref, entry_ref, before_ref, sendx_ref, sendy_ref,
                  state_ref, adjoint_ref, sum_ref):
    k = pl.program_id(0)
    size = heads * width

    @pl.when(k == 0)
    def _():
        state_ref[...] = jnp.zeros_like(state_ref)
        adjoint_ref[...] = jnp.zeros_like(adjoint_ref)
        sum_ref[...] = jnp.zeros_like(sum_ref)

    x_t = x_ref[...].astype(F32).T
    dy_t = dy_ref[...].astype(F32).T
    xt_ref[...] = x_t.astype(BF16)
    dyt_ref[...] = dy_t.astype(BF16)
    rows, columns = indices()
    cum = sums(a_ref[...], (rows <= columns).astype(F32))
    cum_ref[...] = cum
    last = cum[:, SPAN - 1:]
    head_decay = jnp.exp(cum)
    tail = jnp.exp(last - cum)
    scaled, weighted = [], []
    for h in range(heads):
        part = slice(h * width, (h + 1) * width)
        scaled.append((x_t[part] * tail[h:h + 1]).astype(BF16))
        weighted.append((dy_t[part] * head_decay[h:h + 1]).astype(BF16))
    update = mm(jnp.concatenate(scaled, axis=0), b_ref[...], NN)
    own = mm(jnp.concatenate(weighted, axis=0), c_ref[...], NN)
    before = sum_ref[...]
    before_ref[0] = jnp.exp(before)
    entry_ref[0] = state_ref[...]
    for h in range(heads):
        part = slice(h * width, (h + 1) * width)
        state_ref[part] = state_ref[part] * jnp.exp(last[h:h + 1]) + update[part]
        adjoint_ref[part] = adjoint_ref[part] + jnp.exp(before[h:h + 1]) * own[part]
    sum_ref[...] = before + last

    @pl.when(k == pl.num_programs(0) - 1)
    def _():
        for send_ref, place in ((sendx_ref, 0), (sendy_ref, 1)):
            send_ref[:size] = jnp.where(role_ref[place] == 1, state_ref[...], adjoint_ref[...])
            send_ref[size:] = jnp.zeros_like(send_ref[size:])
            send_ref[size:size + heads] = before + last


def local_kernel(heads, width, held, xt_ref, dyt_ref, cum_ref, b_ref, c_ref, *rest):
    inner_ref, back_ref, gain_ref, gbc_ref, skip_ref, gs_ref = rest[held:]
    state_size = b_ref.shape[1]

    @pl.when(pl.program_id(0) == 0)
    def _():
        skip_ref[...] = jnp.zeros_like(skip_ref)

    rows, columns = indices()
    lower = rows <= columns
    cum = cum_ref[...]
    cum_columns = jnp.concatenate(
        [cum, jnp.zeros((-heads % 8, SPAN), F32)] if heads % 8 else [cum], axis=0).T
    b, c = b_ref[...], c_ref[...]
    scores = mm(b, c, NT)
    gain, skip = [], []
    for h in range(heads):
        part = slice(h * width, (h + 1) * width)
        weights = jnp.where(lower, jnp.exp(cum[h:h + 1] - cum_columns[:, h:h + 1]), 0.0)
        mixing = (weights * scores).astype(BF16)
        x_half, dy_half = xt_ref[part], dyt_ref[part]
        inner = mm(x_half, mixing, NN)
        back = mm(dy_half, mixing, NT)
        piece = weights * mm(x_half, dy_half, TN)
        if h == 0:
            gs_ref[...] = piece
        else:
            gs_ref[...] += piece
        x, dy = x_half.astype(F32), dy_half.astype(F32)
        inner_ref[part] = inner
        back_ref[part] = back
        gain.append(jnp.sum(dy * inner - x * back, axis=0, keepdims=True))
        skip.append(jnp.sum(x * dy, axis=0, keepdims=True))
    gain_ref[...] = jnp.concatenate(gain, axis=0)
    skip_ref[...] += jnp.concatenate(skip, axis=0)
    gs_half = gs_ref[...].astype(BF16)
    gbc_ref[:, :state_size] = mm(gs_half, c, NN)
    gbc_ref[:, state_size:] = mm(gs_half, b, TN)


def maps_kernel(heads, width, xt_ref, dyt_ref, cum_ref, c_ref, local_ref, before_ref,
                part_ref, role_ref, *rest):
    received, rest = rest[:-9], rest[-9:]
    (gbc_ref, state_ref, adjoint_ref, edge_ref,
     adj_ref, st_ref, scaled_ref, weighted_ref, entry_ref) = rest
    size = heads * width
    state_size = c_ref.shape[1]

    @pl.when(pl.program_id(0) == 0)
    def _():
        if len(received) == 2:
            entry_ref[...] = received[0][...]
            adj_ref[...] = received[1][...]
            return
        near_ref, side_ref, farx_ref, fary_ref = received
        mine = role_ref[2]
        for h in range(heads):
            part = slice(h * width, (h + 1) * width)
            row = slice(size + h, size + h + 1)
            near, side = near_ref[part], side_ref[part]
            far = farx_ref[part] + fary_ref[part]
            near_sum, side_sum = near_ref[row], side_ref[row]
            far_sum = farx_ref[row] + fary_ref[row]
            whole = near + jnp.exp(near_sum) * side + jnp.exp(near_sum + side_sum) * far
            double = far + jnp.exp(far_sum) * side
            zero = jnp.zeros_like(near)
            entry_ref[part] = jnp.where(
                mine == 0, zero, jnp.where(mine == 1, near, jnp.where(mine == 2, double, whole)))
            adj_ref[part] = jnp.where(
                mine == 3, zero, jnp.where(mine == 2, near, jnp.where(mine == 1, double, whole)))

    cum = cum_ref[...]
    last = cum[:, SPAN - 1:]
    head_decay = jnp.exp(cum)
    tail = jnp.exp(last - cum)
    whole = jnp.exp(last)
    before = before_ref[0]
    edge = []
    for h in range(heads):
        part = slice(h * width, (h + 1) * width)
        state = local_ref[0, part] + before[h:h + 1] * entry_ref[part]
        st_ref[part] = state.astype(BF16)
        products = jnp.sum(state * adj_ref[part], axis=0, keepdims=True)
        edge.append(jnp.sum(products, axis=1, keepdims=True) * whole[h:h + 1])
        scaled_ref[part] = (xt_ref[part].astype(F32) * tail[h:h + 1]).astype(BF16)
        weighted_ref[part] = (dyt_ref[part].astype(F32) * head_decay[h:h + 1]).astype(BF16)
    state_half = st_ref[...]
    adj_half = adj_ref[...].astype(BF16)
    state_ref[0] = state_half
    adjoint_ref[0] = adj_half
    edge_ref[0] = jnp.broadcast_to(jnp.concatenate(edge, axis=0), edge_ref.shape[1:])
    gbc_ref[:, :state_size] = part_ref[:, :state_size] + mm(scaled_ref[...], adj_half, TN)
    gbc_ref[:, state_size:] = part_ref[:, state_size:] + mm(weighted_ref[...], state_half, TN)
    own = mm(weighted_ref[...], c_ref[...], NN)
    for h in range(heads):
        part = slice(h * width, (h + 1) * width)
        adj_ref[part] = adj_ref[part] * whole[h:h + 1] + own[part]


def output_kernel(heads, width, xt_ref, dyt_ref, a_ref, cum_ref, b_ref, c_ref, inner_ref, back_ref,
                  gain_ref, state_ref, adjoint_ref, edge_ref,
                  y_ref, gx_ref, ga_ref, rate_ref, yt_ref, gxt_ref):
    @pl.when(pl.program_id(0) == 0)
    def _():
        rate_ref[...] = jnp.zeros_like(rate_ref)

    rows, columns = indices()
    cum = cum_ref[...]
    last = cum[:, SPAN - 1:]
    head_decay = jnp.exp(cum)
    tail = jnp.exp(last - cum)
    carried_all = mm(state_ref[0], c_ref[...], NT)
    scaled_grad_all = mm(adjoint_ref[0], b_ref[...], NT)
    gain, loss = [], []
    for h in range(heads):
        part = slice(h * width, (h + 1) * width)
        x, dy = xt_ref[part].astype(F32), dyt_ref[part].astype(F32)
        carried = carried_all[part] * head_decay[h:h + 1]
        tailed = scaled_grad_all[part] * tail[h:h + 1]
        yt_ref[part] = inner_ref[part] + carried + x
        gxt_ref[part] = back_ref[part] + tailed + dy
        gain.append(jnp.sum(dy * carried, axis=0, keepdims=True))
        loss.append(jnp.sum(x * tailed, axis=0, keepdims=True))
    y_ref[...] = yt_ref[...].T
    gx_ref[...] = gxt_ref[...].T
    grad = (sums(gain_ref[...] + jnp.concatenate(gain, axis=0), (rows >= columns).astype(F32))
            + sums(jnp.concatenate(loss, axis=0), (rows < columns).astype(F32))
            + edge_ref[0][:, :1])
    ga_ref[...] = grad
    rate_ref[...] += grad * a_ref[...]


def gathered(state, adjoint, heads, width, n):
    size = heads * width
    count, mine = lax.axis_size("seq"), lax.axis_index("seq")
    packed = jnp.concatenate([state[:size], adjoint], axis=0)
    pieces = lax.all_gather(packed, "seq")
    totals = pieces[:, 2 * size:2 * size + heads, 0]
    states = pieces[:, :size].reshape(count, heads, width, n)
    adjoints = pieces[:, size:2 * size].reshape(count, heads, width, n)
    place = jnp.arange(count)
    mid = place[None, :]
    ahead = (mid > place[:, None]) & (mid < mine)
    behind = (mid < place[:, None]) & (mid > mine)
    gap_in = jnp.sum(jnp.where(ahead[:, :, None], totals[None], 0.0), axis=1)
    gap_out = jnp.sum(jnp.where(behind[:, :, None], totals[None], 0.0), axis=1)
    weight_in = jnp.where((place < mine)[:, None], jnp.exp(gap_in), 0.0)
    weight_out = jnp.where((place > mine)[:, None], jnp.exp(gap_out), 0.0)
    entry = jnp.sum(weight_in[:, :, None, None] * states, axis=0).reshape(size, n)
    after = jnp.sum(weight_out[:, :, None, None] * adjoints, axis=0).reshape(size, n)
    return entry, after


def first_round(send_x, send_y):
    by_x = lax.ppermute(send_x, "seq", [(0, 1), (1, 0), (2, 3), (3, 2)])
    by_y = lax.ppermute(send_y, "seq", [(0, 2), (2, 0), (1, 3), (3, 1)])
    return by_x, by_y


def second_round(by_x, by_y):
    far_x = lax.ppermute(by_y, "seq", [(0, 1), (3, 2)])
    far_y = lax.ppermute(by_x, "seq", [(1, 3), (2, 0)])
    return far_x, far_y


def shards(signal, log_decay, b_matrix, c_matrix, out_grad):
    length, size = signal.shape
    heads = log_decay.shape[0]
    width = size // heads
    n = b_matrix.shape[1]
    blocks = length // SPAN
    padded = -(-(size + heads) // 8) * 8
    meshed = lax.axis_size("seq") == 4
    mine = lax.axis_index("seq")
    if meshed:
        role = jnp.stack([mine % 2 == 0, mine < 2, mine]).astype(jnp.int32)
    else:
        role = jnp.array([1, 0, 0], jnp.int32)
    scalars = pl.BlockSpec(memory_space=pltpu.SMEM)
    anywhere = pl.BlockSpec(memory_space=pl.ANY)
    shape = jax.ShapeDtypeStruct
    params = pltpu.CompilerParams(vmem_limit_bytes=56 * 2**20)

    token = pl.BlockSpec((SPAN, size), lambda k: (k, 0))
    flat = pl.BlockSpec((size, SPAN), lambda k: (0, k))
    decay = pl.BlockSpec((heads, SPAN), lambda k: (0, k))
    maps = pl.BlockSpec((SPAN, n), lambda k: (k, 0))
    xt, dyt, cum, local, before, send_x, send_y = pl.pallas_call(
        functools.partial(states_kernel, heads, width),
        grid=(blocks,),
        in_specs=[scalars, token, token, decay, maps, maps],
        out_specs=[flat, flat, decay,
                   pl.BlockSpec((1, size, n), lambda k: (k, 0, 0)),
                   pl.BlockSpec((1, heads, n), lambda k: (k, 0, 0)),
                   pl.BlockSpec((padded, n), lambda k: (0, 0)),
                   pl.BlockSpec((padded, n), lambda k: (0, 0))],
        out_shape=[shape((size, length), BF16), shape((size, length), BF16),
                   shape((heads, length), F32), shape((blocks, size, n), F32),
                   shape((blocks, heads, n), F32), shape((padded, n), F32),
                   shape((padded, n), F32)],
        scratch_shapes=[pltpu.VMEM((size, n), F32), pltpu.VMEM((size, n), F32),
                        pltpu.VMEM((heads, n), F32)],
        compiler_params=params,
    )(role, signal, out_grad, log_decay, b_matrix, c_matrix)

    def grad_cost(micros):
        return pl.CostEstimate(flops=int(micros * 1.0e9), bytes_accessed=int(micros * 3.0e6),
                               transcendentals=0)

    per_block = pl.BlockSpec((1, heads, n), lambda k: (k, 0, 0))
    once = pl.BlockSpec((heads, SPAN), lambda k: (0, 0))

    def local_part(first, count, held):
        def at(k):
            return k + first

        flat_at = pl.BlockSpec((size, SPAN), lambda k: (0, at(k)))
        decay_at = pl.BlockSpec((heads, SPAN), lambda k: (0, at(k)))
        maps_at = pl.BlockSpec((SPAN, n), lambda k: (at(k), 0))
        pair_at = pl.BlockSpec((SPAN, 2 * n), lambda k: (at(k), 0))
        return pl.pallas_call(
            functools.partial(local_kernel, heads, width, len(held)),
            grid=(count,),
            in_specs=[flat_at, flat_at, decay_at, maps_at, maps_at] + [anywhere] * len(held),
            out_specs=[flat_at, flat_at, decay_at, pair_at, once],
            out_shape=[shape((size, length), F32), shape((size, length), F32),
                       shape((heads, length), F32), shape((length, 2 * n), F32),
                       shape((heads, SPAN), F32)],
            scratch_shapes=[pltpu.VMEM((SPAN, SPAN), F32)],
            input_output_aliases={5 + place: place for place in range(len(held))},
            compiler_params=params, cost_estimate=grad_cost(2 * count),
        )(xt, dyt, cum, b_matrix, c_matrix, *held)

    half = blocks // 2
    if meshed and half:
        by_x, by_y = first_round(send_x, send_y)
        *held, skip_first = local_part(0, half, [])
        by_x, by_y, held = lax.optimization_barrier((by_x, by_y, held))
        far_x, far_y = second_round(by_x, by_y)
        inner, back, gain, local_maps, skip = local_part(half, blocks - half, held)
        skip = skip + skip_first
        received = (by_x, by_y, far_x, far_y)
    else:
        inner, back, gain, local_maps, skip = local_part(0, blocks, [])
        received = gathered(send_x, send_y, heads, width, n)

    end = blocks - 1
    r_flat = pl.BlockSpec((size, SPAN), lambda k: (0, end - k))
    r_state = pl.BlockSpec((1, size, n), lambda k: (end - k, 0, 0))
    r_block = pl.BlockSpec((1, heads, n), lambda k: (end - k, 0, 0))
    r_pair = pl.BlockSpec((SPAN, 2 * n), lambda k: (end - k, 0))
    whole_specs = [pl.BlockSpec(value.shape, lambda k: (0, 0)) for value in received]
    gbc, state_half, adj_half, edge = pl.pallas_call(
        functools.partial(maps_kernel, heads, width),
        grid=(blocks,),
        in_specs=[r_flat, r_flat, pl.BlockSpec((heads, SPAN), lambda k: (0, end - k)),
                  pl.BlockSpec((SPAN, n), lambda k: (end - k, 0)), r_state, r_block,
                  r_pair, scalars] + whole_specs,
        out_specs=[r_pair, r_state, r_state, r_block],
        out_shape=[shape((length, 2 * n), F32), shape((blocks, size, n), BF16),
                   shape((blocks, size, n), BF16), shape((blocks, heads, n), F32)],
        scratch_shapes=[pltpu.VMEM((size, n), F32), pltpu.VMEM((size, n), BF16),
                        pltpu.VMEM((size, SPAN), BF16), pltpu.VMEM((size, SPAN), BF16),
                        pltpu.VMEM((size, n), F32)],
        compiler_params=params, cost_estimate=grad_cost(6),
    )(xt, dyt, cum, c_matrix, local, before, local_maps, role, *received)

    shared = lax.psum_scatter(gbc, "head", scatter_dimension=0, tiled=True)

    state_spec = pl.BlockSpec((1, size, n), lambda k: (k, 0, 0))
    y, gx, ga, rate = pl.pallas_call(
        functools.partial(output_kernel, heads, width),
        grid=(blocks,),
        in_specs=[flat, flat, decay, decay, maps, maps, flat, flat, decay,
                  state_spec, state_spec, per_block],
        out_specs=[token, token, decay, once],
        out_shape=[shape((length, size), F32), shape((length, size), F32),
                   shape((heads, length), F32), shape((heads, SPAN), F32)],
        scratch_shapes=[pltpu.VMEM((size, SPAN), F32), pltpu.VMEM((size, SPAN), F32)],
        compiler_params=params, cost_estimate=grad_cost(14),
    )(xt, dyt, log_decay, cum, b_matrix, c_matrix, inner, back, gain, state_half, adj_half, edge)

    head_grads = lax.psum(jnp.stack([jnp.sum(skip, axis=1), jnp.sum(rate, axis=1)]), "seq")
    return y, gx, ga, shared[:, :n], shared[:, n:], head_grads


def solution(mesh):
    in_specs = (
        P("seq", "head"),
        P("head", "seq"),
        P("seq", None),
        P("seq", None),
        P("seq", "head"),
    )
    out_specs = (
        P("seq", "head"),
        P("seq", "head"),
        P("head", "seq"),
        P(("seq", "head"), None),
        P(("seq", "head"), None),
        P(None, "head"),
    )
    return jax.shard_map(shards, mesh=mesh, in_specs=in_specs, out_specs=out_specs, check_vma=False)
```

```python
import functools

import jax
import jax.numpy as jnp
from jax import lax
from jax.experimental import pallas as pl
from jax.experimental.pallas import tpu as pltpu
from jax.sharding import PartitionSpec as P

SPAN = 256
F32 = jnp.float32
BF16 = jnp.bfloat16
NN = (((1,), (0,)), ((), ()))
NT = (((1,), (1,)), ((), ()))
TN = (((0,), (0,)), ((), ()))


def mm(left, right, dims):
    return lax.dot_general(left, right, dims, preferred_element_type=F32)


def sums(left, right):
    return jnp.dot(left, right, precision=lax.Precision.HIGHEST, preferred_element_type=F32)


def indices():
    rows = lax.broadcasted_iota(jnp.int32, (SPAN, SPAN), 0)
    columns = lax.broadcasted_iota(jnp.int32, (SPAN, SPAN), 1)
    return rows, columns


def states_kernel(heads, width, role_ref, x_ref, dy_ref, a_ref, b_ref, c_ref,
                  xt_ref, dyt_ref, cum_ref, entry_ref, before_ref, sendx_ref, sendy_ref,
                  state_ref, adjoint_ref, sum_ref):
    k = pl.program_id(0)
    size = heads * width

    @pl.when(k == 0)
    def _():
        state_ref[...] = jnp.zeros_like(state_ref)
        adjoint_ref[...] = jnp.zeros_like(adjoint_ref)
        sum_ref[...] = jnp.zeros_like(sum_ref)

    x_t = x_ref[...].astype(F32).T
    dy_t = dy_ref[...].astype(F32).T
    xt_ref[...] = x_t.astype(BF16)
    dyt_ref[...] = dy_t.astype(BF16)
    rows, columns = indices()
    cum = sums(a_ref[...], (rows <= columns).astype(F32))
    cum_ref[...] = cum
    last = cum[:, SPAN - 1:]
    head_decay = jnp.exp(cum)
    tail = jnp.exp(last - cum)
    scaled, weighted = [], []
    for h in range(heads):
        part = slice(h * width, (h + 1) * width)
        scaled.append((x_t[part] * tail[h:h + 1]).astype(BF16))
        weighted.append((dy_t[part] * head_decay[h:h + 1]).astype(BF16))
    update = mm(jnp.concatenate(scaled, axis=0), b_ref[...], NN)
    own = mm(jnp.concatenate(weighted, axis=0), c_ref[...], NN)
    before = sum_ref[...]
    before_ref[0] = jnp.exp(before)
    entry_ref[0] = state_ref[...]
    for h in range(heads):
        part = slice(h * width, (h + 1) * width)
        state_ref[part] = state_ref[part] * jnp.exp(last[h:h + 1]) + update[part]
        adjoint_ref[part] = adjoint_ref[part] + jnp.exp(before[h:h + 1]) * own[part]
    sum_ref[...] = before + last

    @pl.when(k == pl.num_programs(0) - 1)
    def _():
        for send_ref, place in ((sendx_ref, 0), (sendy_ref, 1)):
            send_ref[:size] = jnp.where(role_ref[place] == 1, state_ref[...], adjoint_ref[...])
            send_ref[size:] = jnp.zeros_like(send_ref[size:])
            send_ref[size:size + heads] = before + last


def local_kernel(heads, width, held, xt_ref, dyt_ref, cum_ref, b_ref, c_ref, *rest):
    inner_ref, back_ref, gain_ref, gbc_ref, skip_ref, gs_ref = rest[held:]
    state_size = b_ref.shape[1]

    @pl.when(pl.program_id(0) == 0)
    def _():
        skip_ref[...] = jnp.zeros_like(skip_ref)

    rows, columns = indices()
    lower = rows <= columns
    cum = cum_ref[...]
    cum_columns = jnp.concatenate(
        [cum, jnp.zeros((-heads % 8, SPAN), F32)] if heads % 8 else [cum], axis=0).T
    b, c = b_ref[...], c_ref[...]
    scores = mm(b, c, NT)
    gain, skip = [], []
    for h in range(heads):
        part = slice(h * width, (h + 1) * width)
        weights = jnp.where(lower, jnp.exp(cum[h:h + 1] - cum_columns[:, h:h + 1]), 0.0)
        mixing = (weights * scores).astype(BF16)
        x_half, dy_half = xt_ref[part], dyt_ref[part]
        inner = mm(x_half, mixing, NN)
        back = mm(dy_half, mixing, NT)
        piece = weights * mm(x_half, dy_half, TN)
        if h == 0:
            gs_ref[...] = piece
        else:
            gs_ref[...] += piece
        x, dy = x_half.astype(F32), dy_half.astype(F32)
        inner_ref[part] = inner
        back_ref[part] = back
        gain.append(jnp.sum(dy * inner - x * back, axis=0, keepdims=True))
        skip.append(jnp.sum(x * dy, axis=0, keepdims=True))
    gain_ref[...] = jnp.concatenate(gain, axis=0)
    skip_ref[...] += jnp.concatenate(skip, axis=0)
    gs_half = gs_ref[...].astype(BF16)
    gbc_ref[:, :state_size] = mm(gs_half, c, NN)
    gbc_ref[:, state_size:] = mm(gs_half, b, TN)


def maps_kernel(heads, width, xt_ref, dyt_ref, cum_ref, c_ref, local_ref, before_ref,
                part_ref, role_ref, *rest):
    received, rest = rest[:-8], rest[-8:]
    (gbc_ref, state_ref, adjoint_ref,
     adj_ref, st_ref, scaled_ref, weighted_ref, entry_ref) = rest
    size = heads * width
    state_size = c_ref.shape[1]

    @pl.when(pl.program_id(0) == 0)
    def _():
        if len(received) == 2:
            entry_ref[...] = received[0][...]
            adj_ref[...] = received[1][...]
            return
        near_ref, side_ref, farx_ref, fary_ref = received
        mine = role_ref[2]
        for h in range(heads):
            part = slice(h * width, (h + 1) * width)
            row = slice(size + h, size + h + 1)
            near, side = near_ref[part], side_ref[part]
            far = farx_ref[part] + fary_ref[part]
            near_sum, side_sum = near_ref[row], side_ref[row]
            far_sum = farx_ref[row] + fary_ref[row]
            whole = near + jnp.exp(near_sum) * side + jnp.exp(near_sum + side_sum) * far
            double = far + jnp.exp(far_sum) * side
            zero = jnp.zeros_like(near)
            entry_ref[part] = jnp.where(
                mine == 0, zero, jnp.where(mine == 1, near, jnp.where(mine == 2, double, whole)))
            adj_ref[part] = jnp.where(
                mine == 3, zero, jnp.where(mine == 2, near, jnp.where(mine == 1, double, whole)))

    cum = cum_ref[...]
    last = cum[:, SPAN - 1:]
    head_decay = jnp.exp(cum)
    tail = jnp.exp(last - cum)
    whole = jnp.exp(last)
    before = before_ref[0]
    for h in range(heads):
        part = slice(h * width, (h + 1) * width)
        state = local_ref[0, part] + before[h:h + 1] * entry_ref[part]
        st_ref[part] = state.astype(BF16)
        scaled_ref[part] = (xt_ref[part].astype(F32) * tail[h:h + 1]).astype(BF16)
        weighted_ref[part] = (dyt_ref[part].astype(F32) * head_decay[h:h + 1]).astype(BF16)
    state_half = st_ref[...]
    adj_half = adj_ref[...].astype(BF16)
    state_ref[0] = state_half
    adjoint_ref[0] = adj_half
    gbc_ref[:, :state_size] = part_ref[:, :state_size] + mm(adj_half, scaled_ref[...], TN).T
    gbc_ref[:, state_size:] = part_ref[:, state_size:] + mm(state_half, weighted_ref[...], TN).T
    own = mm(weighted_ref[...], c_ref[...], NN)
    for h in range(heads):
        part = slice(h * width, (h + 1) * width)
        adj_ref[part] = adj_ref[part] * whole[h:h + 1] + own[part]


def output_kernel(heads, width, xt_ref, dyt_ref, a_ref, cum_ref, b_ref, c_ref, inner_ref, back_ref,
                  gain_ref, state_ref, adjoint_ref,
                  y_ref, gx_ref, ga_ref, rate_ref, yt_ref, gxt_ref):
    @pl.when(pl.program_id(0) == 0)
    def _():
        rate_ref[...] = jnp.zeros_like(rate_ref)

    rows, columns = indices()
    cum = cum_ref[...]
    last = cum[:, SPAN - 1:]
    head_decay = jnp.exp(cum)
    tail = jnp.exp(last - cum)
    carried_all = mm(state_ref[0], c_ref[...], NT)
    scaled_grad_all = mm(adjoint_ref[0], b_ref[...], NT)
    gain, loss, edge = [], [], []
    for h in range(heads):
        part = slice(h * width, (h + 1) * width)
        x, dy = xt_ref[part].astype(F32), dyt_ref[part].astype(F32)
        carried = carried_all[part] * head_decay[h:h + 1]
        tailed = scaled_grad_all[part] * tail[h:h + 1]
        yt_ref[part] = inner_ref[part] + carried + x
        gxt_ref[part] = back_ref[part] + tailed + dy
        gain.append(jnp.sum(dy * carried, axis=0, keepdims=True))
        loss.append(jnp.sum(x * tailed, axis=0, keepdims=True))
        edge.append(jnp.sum(state_ref[0, part].astype(F32) * adjoint_ref[0, part].astype(F32),
                            axis=0, keepdims=True))
    y_ref[...] = yt_ref[...].T
    gx_ref[...] = gxt_ref[...].T
    grad = (sums(gain_ref[...] + jnp.concatenate(gain, axis=0), (rows >= columns).astype(F32))
            + sums(jnp.concatenate(loss, axis=0), (rows < columns).astype(F32))
            + jnp.exp(last) * jnp.sum(jnp.concatenate(edge, axis=0), axis=1, keepdims=True))
    ga_ref[...] = grad
    rate_ref[...] += grad * a_ref[...]


def gathered(state, adjoint, heads, width, n):
    size = heads * width
    count, mine = lax.axis_size("seq"), lax.axis_index("seq")
    packed = jnp.concatenate([state[:size], adjoint], axis=0)
    pieces = lax.all_gather(packed, "seq")
    totals = pieces[:, 2 * size:2 * size + heads, 0]
    states = pieces[:, :size].reshape(count, heads, width, n)
    adjoints = pieces[:, size:2 * size].reshape(count, heads, width, n)
    place = jnp.arange(count)
    mid = place[None, :]
    ahead = (mid > place[:, None]) & (mid < mine)
    behind = (mid < place[:, None]) & (mid > mine)
    gap_in = jnp.sum(jnp.where(ahead[:, :, None], totals[None], 0.0), axis=1)
    gap_out = jnp.sum(jnp.where(behind[:, :, None], totals[None], 0.0), axis=1)
    weight_in = jnp.where((place < mine)[:, None], jnp.exp(gap_in), 0.0)
    weight_out = jnp.where((place > mine)[:, None], jnp.exp(gap_out), 0.0)
    entry = jnp.sum(weight_in[:, :, None, None] * states, axis=0).reshape(size, n)
    after = jnp.sum(weight_out[:, :, None, None] * adjoints, axis=0).reshape(size, n)
    return entry, after


def first_round(send_x, send_y):
    by_x = lax.ppermute(send_x, "seq", [(0, 1), (1, 0), (2, 3), (3, 2)])
    by_y = lax.ppermute(send_y, "seq", [(0, 2), (2, 0), (1, 3), (3, 1)])
    return by_x, by_y


def second_round(by_x, by_y):
    far_x = lax.ppermute(by_y, "seq", [(0, 1), (3, 2)])
    far_y = lax.ppermute(by_x, "seq", [(1, 3), (2, 0)])
    return far_x, far_y


def shards(signal, log_decay, b_matrix, c_matrix, out_grad):
    length, size = signal.shape
    heads = log_decay.shape[0]
    width = size // heads
    n = b_matrix.shape[1]
    blocks = length // SPAN
    padded = -(-(size + heads) // 8) * 8
    meshed = lax.axis_size("seq") == 4
    mine = lax.axis_index("seq")
    if meshed:
        role = jnp.stack([mine % 2 == 0, mine < 2, mine]).astype(jnp.int32)
    else:
        role = jnp.array([1, 0, 0], jnp.int32)
    scalars = pl.BlockSpec(memory_space=pltpu.SMEM)
    anywhere = pl.BlockSpec(memory_space=pl.ANY)
    shape = jax.ShapeDtypeStruct
    params = pltpu.CompilerParams(vmem_limit_bytes=56 * 2**20)

    token = pl.BlockSpec((SPAN, size), lambda k: (k, 0))
    flat = pl.BlockSpec((size, SPAN), lambda k: (0, k))
    decay = pl.BlockSpec((heads, SPAN), lambda k: (0, k))
    maps = pl.BlockSpec((SPAN, n), lambda k: (k, 0))
    xt, dyt, cum, local, before, send_x, send_y = pl.pallas_call(
        functools.partial(states_kernel, heads, width),
        grid=(blocks,),
        in_specs=[scalars, token, token, decay, maps, maps],
        out_specs=[flat, flat, decay,
                   pl.BlockSpec((1, size, n), lambda k: (k, 0, 0)),
                   pl.BlockSpec((1, heads, n), lambda k: (k, 0, 0)),
                   pl.BlockSpec((padded, n), lambda k: (0, 0)),
                   pl.BlockSpec((padded, n), lambda k: (0, 0))],
        out_shape=[shape((size, length), BF16), shape((size, length), BF16),
                   shape((heads, length), F32), shape((blocks, size, n), F32),
                   shape((blocks, heads, n), F32), shape((padded, n), F32),
                   shape((padded, n), F32)],
        scratch_shapes=[pltpu.VMEM((size, n), F32), pltpu.VMEM((size, n), F32),
                        pltpu.VMEM((heads, n), F32)],
        compiler_params=params,
    )(role, signal, out_grad, log_decay, b_matrix, c_matrix)

    def grad_cost(micros):
        return pl.CostEstimate(flops=int(micros * 1.0e9), bytes_accessed=int(micros * 3.0e6),
                               transcendentals=0)

    once = pl.BlockSpec((heads, SPAN), lambda k: (0, 0))

    def local_part(first, count, held):
        def at(k):
            return k + first

        flat_at = pl.BlockSpec((size, SPAN), lambda k: (0, at(k)))
        decay_at = pl.BlockSpec((heads, SPAN), lambda k: (0, at(k)))
        maps_at = pl.BlockSpec((SPAN, n), lambda k: (at(k), 0))
        pair_at = pl.BlockSpec((SPAN, 2 * n), lambda k: (at(k), 0))
        return pl.pallas_call(
            functools.partial(local_kernel, heads, width, len(held)),
            grid=(count,),
            in_specs=[flat_at, flat_at, decay_at, maps_at, maps_at] + [anywhere] * len(held),
            out_specs=[flat_at, flat_at, decay_at, pair_at, once],
            out_shape=[shape((size, length), F32), shape((size, length), F32),
                       shape((heads, length), F32), shape((length, 2 * n), F32),
                       shape((heads, SPAN), F32)],
            scratch_shapes=[pltpu.VMEM((SPAN, SPAN), F32)],
            input_output_aliases={5 + place: place for place in range(len(held))},
            compiler_params=params, cost_estimate=grad_cost(2 * count),
        )(xt, dyt, cum, b_matrix, c_matrix, *held)

    half = blocks // 2
    if meshed and half:
        by_x, by_y = first_round(send_x, send_y)
        *held, skip_first = local_part(0, half, [])
        by_x, by_y, held = lax.optimization_barrier((by_x, by_y, held))
        far_x, far_y = second_round(by_x, by_y)
        inner, back, gain, local_maps, skip = local_part(half, blocks - half, held)
        skip = skip + skip_first
        received = (by_x, by_y, far_x, far_y)
    else:
        inner, back, gain, local_maps, skip = local_part(0, blocks, [])
        received = gathered(send_x, send_y, heads, width, n)

    end = blocks - 1
    r_flat = pl.BlockSpec((size, SPAN), lambda k: (0, end - k))
    r_state = pl.BlockSpec((1, size, n), lambda k: (end - k, 0, 0))
    r_block = pl.BlockSpec((1, heads, n), lambda k: (end - k, 0, 0))
    r_pair = pl.BlockSpec((SPAN, 2 * n), lambda k: (end - k, 0))
    whole_specs = [pl.BlockSpec(value.shape, lambda k: (0, 0)) for value in received]
    gbc, state_half, adj_half = pl.pallas_call(
        functools.partial(maps_kernel, heads, width),
        grid=(blocks,),
        in_specs=[r_flat, r_flat, pl.BlockSpec((heads, SPAN), lambda k: (0, end - k)),
                  pl.BlockSpec((SPAN, n), lambda k: (end - k, 0)), r_state, r_block,
                  r_pair, scalars] + whole_specs,
        out_specs=[r_pair, r_state, r_state],
        out_shape=[shape((length, 2 * n), F32), shape((blocks, size, n), BF16),
                   shape((blocks, size, n), BF16)],
        scratch_shapes=[pltpu.VMEM((size, n), F32), pltpu.VMEM((size, n), BF16),
                        pltpu.VMEM((size, SPAN), BF16), pltpu.VMEM((size, SPAN), BF16),
                        pltpu.VMEM((size, n), F32)],
        compiler_params=params, cost_estimate=grad_cost(6),
    )(xt, dyt, cum, c_matrix, local, before, local_maps, role, *received)

    shared = lax.psum_scatter(gbc, "head", scatter_dimension=0, tiled=True)

    state_spec = pl.BlockSpec((1, size, n), lambda k: (k, 0, 0))
    y, gx, ga, rate = pl.pallas_call(
        functools.partial(output_kernel, heads, width),
        grid=(blocks,),
        in_specs=[flat, flat, decay, decay, maps, maps, flat, flat, decay,
                  state_spec, state_spec],
        out_specs=[token, token, decay, once],
        out_shape=[shape((length, size), F32), shape((length, size), F32),
                   shape((heads, length), F32), shape((heads, SPAN), F32)],
        scratch_shapes=[pltpu.VMEM((size, SPAN), F32), pltpu.VMEM((size, SPAN), F32)],
        compiler_params=params, cost_estimate=grad_cost(14),
    )(xt, dyt, log_decay, cum, b_matrix, c_matrix, inner, back, gain, state_half, adj_half)

    head_grads = lax.psum(jnp.stack([jnp.sum(skip, axis=1), jnp.sum(rate, axis=1)]), "seq")
    return y, gx, ga, shared[:, :n], shared[:, n:], head_grads


def solution(mesh):
    in_specs = (
        P("seq", "head"),
        P("head", "seq"),
        P("seq", None),
        P("seq", None),
        P("seq", "head"),
    )
    out_specs = (
        P("seq", "head"),
        P("seq", "head"),
        P("head", "seq"),
        P(("seq", "head"), None),
        P(("seq", "head"), None),
        P(None, "head"),
    )
    return jax.shard_map(shards, mesh=mesh, in_specs=in_specs, out_specs=out_specs, check_vma=False)
```
